128 devices in a mesh: section: 4 (over y), seq: 8 (over x, core), tp: 4 (over z).
Axes of the slice: x: 4, y: 4, z: 4, core: 2. Of those that a mesh axis runs over, the one named last changes fastest.
Arguments:
- queries: bfloat16 [12288, 4096], P(('section', 'seq'), 'tp'), may hold values from -200 to 200
- neighbours: bfloat16 [49152, 4096], P(('section', 'seq'), 'tp'), may hold values from -400 to 400
- norm_gain: float32 [4096], replicated, may hold values from 0.1 to 1.9
- key_weight: bfloat16 [4, 4096, 4096], P('section', None, 'tp'), may hold values from -0.09375 to 0.09375
- value_weight: bfloat16 [4, 4096, 4096], P('section', None, 'tp'), may hold values from -0.09375 to 0.09375
- slot_anchor: int32 [768], P(('section', 'seq')), may hold values from 0 to 767, as said below
- nbr_count: int32 [192], P(('section', 'seq')), may hold values from 1 to 2, as said below
Outputs:
- attended: bfloat16 [12288, 4096], P(('section', 'seq'), 'tp')
The draws below stay inside these ranges and needn't reach their ends.
Inputs may be any that keep to these rules, and one draw needn't show every extreme that they name: `slot_anchor`: every piece fills exactly one slot. The slots of one block name pieces of exactly 12 blocks, two pieces from each. `nbr_count`: how many of a stretch's neighbours are usable; some blocks have far more usable neighbours than others.
All inputs are finite; a program needn't handle non-finite values.
Results may differ from the reference program's by a relative error of at most 0.004.
The reference program's roundings to bfloat16 on the way count: a program that leaves them out, or rounds other values in their place, can miss the bound.
Values may be sent and summed in bfloat16 or wider, within the bound.
No kernel may reach another device: no remote copies, remote signals or barrier semaphores. Data moves between devices by JAX's collectives and lax.ppermute only.
A program may use at most 128 MiB of HBM per device.

```python
import jax
import jax.numpy as jnp
from jax import lax

D = 4096
HEADS = 32
HD = 128
STRETCH = 64
PIECE = 64
NBR = 2
CH_DEV = 6
TOK_DEV = 384
UNITS_DEV = 24
OWNERS = 32
TOKENS = 12288
UNITS = 768
SECTIONS = 4
N_SEQ = 8


def shuffle_units(subkey):
    return jax.random.permutation(subkey, UNITS_DEV)


def draw_slot_anchor(key, part):
    key = jax.random.fold_in(key, 11)
    first_key, second_key, third_key, fourth_key = jax.random.split(key, 4)
    sigma_perm = jax.random.permutation(first_key, OWNERS)
    rho_perm = jax.random.permutation(second_key, OWNERS)
    inverse_sigma = jnp.argsort(sigma_perm)
    inverse_rho = jnp.argsort(rho_perm)
    pair_count = UNITS_DEV // 2
    owner_ids = jnp.arange(OWNERS)[:, None]
    pair_ids = jnp.arange(pair_count)[None, :]
    sender = inverse_sigma[(inverse_rho[owner_ids] - pair_ids) % OWNERS]
    orders = jax.vmap(shuffle_units)(jax.random.split(third_key, OWNERS))
    first_unit = orders[sender, 2 * pair_ids]
    second_unit = orders[sender, 2 * pair_ids + 1]
    units = jnp.stack([sender * UNITS_DEV + first_unit, sender * UNITS_DEV + second_unit], -1).reshape(OWNERS, UNITS_DEV)
    shuffles = jax.vmap(shuffle_units)(jax.random.split(fourth_key, OWNERS))
    return jnp.take_along_axis(units, shuffles, 1).reshape(-1).astype(jnp.int32)


def draw_nbr_count(key, part):
    key = jax.random.fold_in(key, 12)
    first_key, second_key = jax.random.split(key)
    leaning = jax.random.randint(first_key, (OWNERS, 1), 0, 11)
    rolls = jax.random.randint(second_key, (OWNERS, CH_DEV), 0, 10)
    return (1 + (rolls < leaning).astype(jnp.int32)).reshape(-1).astype(jnp.int32)


def draw_queries(key, part):
    key = jax.random.fold_in(key, 13)
    first_key = jax.random.fold_in(key, 0)
    base = jnp.clip(jax.random.normal(first_key, (TOKENS, HEADS * HD), jnp.float32), -4.0, 4.0)
    return base.astype(jnp.bfloat16)


def draw_neighbours(key, part):
    key = jax.random.fold_in(key, 14)
    first_key, second_key, third_key = jax.random.split(key, 3)
    col_scale = jnp.exp(jax.random.uniform(third_key, (1, D), jnp.float32, 0.0, 2.3))
    base = jnp.clip(jax.random.normal(first_key, (UNITS * PIECE, D), jnp.float32), -4.0, 4.0)
    row_scale = jnp.exp(jax.random.uniform(second_key, (UNITS * PIECE, 1), jnp.float32, 0.0, 2.3))
    return (base * row_scale * col_scale).astype(jnp.bfloat16)


def level_of(rng, extent, cuts, least, largest):
    def one(position, shards_of):
        steps = jax.random.uniform(jax.random.fold_in(jax.random.fold_in(rng, 6), position), (shards_of,), jnp.float32, least / len(cuts), largest / len(cuts))
        return jnp.repeat(jnp.exp(steps), extent[position] // shards_of).reshape((-1,) + (1,) * (len(extent) - position - 1))

    factor_of = one(*cuts[0])
    for cut in cuts[1:]:
        factor_of = factor_of * one(*cut)
    return factor_of


def gaussian(rng, dims, deviation, most, cuts=(), kind=jnp.bfloat16):
    drawn = jax.random.normal(rng, dims, jnp.float32) * deviation
    if len(cuts) > 0:
        drawn = level_of(rng, dims, cuts, -0.22, 0.18) * drawn
    return jnp.clip(drawn, min=-most, max=most).astype(kind)


def setup_inputs(seed: int = 0) -> dict:
    keys = jax.random.split(jax.random.key(seed), 8)
    return {
        "queries": draw_queries(jax.random.fold_in(keys[7], 71), 0),
        "neighbours": draw_neighbours(jax.random.fold_in(keys[7], 71), 0),
        "norm_gain": jnp.clip(1.0 + 0.18 * jax.random.normal(keys[2], (D,), jnp.float32), 0.1, 1.9),
        "key_weight": gaussian(keys[3], (SECTIONS, D, HEADS * HD), D ** -0.5, 0.09375, ((0, 4), (2, 4))),
        "value_weight": gaussian(keys[4], (SECTIONS, D, HEADS * HD), D ** -0.5, 0.09375, ((0, 4), (2, 4))),
        "slot_anchor": draw_slot_anchor(jax.random.fold_in(keys[7], 71), 0),
        "nbr_count": draw_nbr_count(jax.random.fold_in(keys[7], 71), 0),
    }


norm_eps = 1e-05

def attend(query_rows, key_rows, value_rows, stretch_counts):
    head_count = query_rows.shape[1] // HD
    key_span = NBR * 2 * PIECE
    query_heads = query_rows.reshape(CH_DEV, STRETCH, head_count, HD).astype(jnp.float32)
    key_heads = key_rows.reshape(CH_DEV, key_span, head_count, HD).astype(jnp.float32)
    value_heads = value_rows.reshape(CH_DEV, key_span, head_count, HD).astype(jnp.float32)
    scores = jnp.einsum('cqhd,ckhd->chqk', query_heads, key_heads) * HD ** (-0.5)
    neighbour_of_key = jnp.arange(key_span, dtype=jnp.int32) // (2 * PIECE)
    usable = neighbour_of_key[None, :] < stretch_counts[:, None]
    scores = jnp.where(usable[:, None, None, :], scores, -1e+30)
    row_max = lax.optimization_barrier(jnp.max(scores, -1, keepdims=True))
    exponents = jnp.exp(scores - row_max)
    weights = (exponents / lax.optimization_barrier(jnp.sum(exponents, -1, keepdims=True))).astype(jnp.bfloat16)
    combined = jnp.einsum('chqk,ckhd->cqhd', weights.astype(jnp.float32), value_heads)
    return combined.astype(jnp.bfloat16).reshape(CH_DEV * STRETCH, head_count * HD)

def reference(queries, neighbours, norm_gain, key_weight, value_weight, slot_anchor, nbr_count):
    pieces = neighbours.reshape(UNITS, PIECE, D)

    def one_owner(owner):
        anchor = lax.dynamic_slice_in_dim(slot_anchor, owner * UNITS_DEV, UNITS_DEV)
        row_values = jnp.take(pieces, anchor, axis=0).reshape(UNITS_DEV * PIECE, D).astype(jnp.float32)
        mean_square = lax.optimization_barrier(jnp.mean(row_values * row_values, -1, keepdims=True))
        encoded = (row_values * lax.rsqrt(mean_square + norm_eps) * norm_gain).astype(jnp.bfloat16)
        layer = owner // N_SEQ
        key_matrix = lax.dynamic_index_in_dim(key_weight, layer, 0, keepdims=False)
        value_matrix = lax.dynamic_index_in_dim(value_weight, layer, 0, keepdims=False)
        key_rows = jnp.dot(encoded, key_matrix, preferred_element_type=jnp.float32).astype(jnp.bfloat16)
        value_rows = jnp.dot(encoded, value_matrix, preferred_element_type=jnp.float32).astype(jnp.bfloat16)
        query_rows = lax.dynamic_slice_in_dim(queries, owner * TOK_DEV, TOK_DEV)
        stretch_counts = lax.dynamic_slice_in_dim(nbr_count, owner * CH_DEV, CH_DEV)
        return attend(query_rows, key_rows, value_rows, stretch_counts)
    results = lax.map(one_owner, jnp.arange(OWNERS, dtype=jnp.int32))
    return results.reshape(TOKENS, HEADS * HD)
```

```python
import functools

import jax
import jax.numpy as jnp
from jax import lax
from jax.experimental import pallas as pl
from jax.experimental.pallas import tpu as pltpu
from jax.sharding import PartitionSpec as P

HD = 128
PIECE = 64
NBR = 2
CHUNKS = (16, 16, 16, 16)
MODE = ("offload", "ring", "offload", "ring")
EPS = 1e-05
OWN = ("section", "seq")
KERNEL_VMEM = 62 << 20


def scatter_rows(position, pieces, offset, rows, cells):
    count, _, width = pieces.shape

    def body(position_ref, pieces_ref, out_ref, held, sem, sems):
        load = pltpu.make_async_copy(pieces_ref.at[:, pl.ds(offset, rows)], held, sem)
        load.start()
        load.wait()

        def copy(u):
            return pltpu.make_async_copy(held.at[u], out_ref.at[position_ref[u]], sems.at[u])

        for u in range(count):
            copy(u).start()
        for u in range(count):
            copy(u).wait()

    return pl.pallas_call(
        body,
        out_shape=jax.ShapeDtypeStruct((cells, rows, width), pieces.dtype),
        in_specs=[pl.BlockSpec(memory_space=pltpu.SMEM), pl.BlockSpec(memory_space=pl.ANY)],
        out_specs=pl.BlockSpec(memory_space=pl.ANY),
        scratch_shapes=[
            pltpu.VMEM((count, rows, width), pieces.dtype),
            pltpu.SemaphoreType.DMA,
            pltpu.SemaphoreType.DMA((count,)),
        ],
        compiler_params=pltpu.CompilerParams(vmem_limit_bytes=KERNEL_VMEM),
        cost_estimate=pl.CostEstimate(flops=0, bytes_accessed=4 * count * rows * width, transcendentals=0),
        name="pick_rows",
    )(position, pieces)


def gather_rows(position, cells):
    count = position.shape[0]
    _, rows, width = cells.shape

    def body(position_ref, cells_ref, out_ref, held, sem, sems):
        def copy(t):
            return pltpu.make_async_copy(cells_ref.at[position_ref[t]], held.at[t], sems.at[t])

        for t in range(count):
            copy(t).start()
        for t in range(count):
            copy(t).wait()
        store = pltpu.make_async_copy(held, out_ref, sem)
        store.start()
        store.wait()

    return pl.pallas_call(
        body,
        out_shape=jax.ShapeDtypeStruct((count, rows, width), cells.dtype),
        in_specs=[pl.BlockSpec(memory_space=pltpu.SMEM), pl.BlockSpec(memory_space=pl.ANY)],
        out_specs=pl.BlockSpec(memory_space=pl.ANY),
        scratch_shapes=[
            pltpu.VMEM((count, rows, width), cells.dtype),
            pltpu.SemaphoreType.DMA,
            pltpu.SemaphoreType.DMA((count,)),
        ],
        compiler_params=pltpu.CompilerParams(vmem_limit_bytes=KERNEL_VMEM),
        cost_estimate=pl.CostEstimate(flops=0, bytes_accessed=4 * count * rows * width, transcendentals=0),
        name="place_rows",
    )(position, cells)


def after(x, *others):
    return lax.optimization_barrier((x,) + others)[0]


def send(x, step):
    size = lax.axis_size("tp")
    return lax.ppermute(x, "tp", [(i, (i + step) % size) for i in range(size)])


def project(parts, gain, key_matrix, value_matrix):
    if parts[-1][0] is None:
        parts = parts[1:]
    rows, width = parts[0][2].shape[-2:]
    depth, columns = key_matrix.shape
    size = depth // width
    tile = 256
    block = 16
    here = lax.axis_index("tp").astype(jnp.int32).reshape(1)
    n = len(parts)

    def body(here_ref, gain_ref, key_ref, value_ref, *refs):
        part_refs, key_out, value_out, encoded = refs[:n], refs[n], refs[n + 1], refs[n + 2]

        @pl.when(pl.program_id(0) == 0)
        def _():
            def group(first, last, some):
                def load(ref, at, start):
                    return ref[pl.ds(pl.multiple_of(at - start, block), block), :].astype(jnp.float32)

                def place_of(step):
                    if isinstance(step, tuple):
                        return slice(step[0] * width, (step[0] + 1) * width)
                    return pl.ds(pl.multiple_of((here_ref[0] + step) % size * width, width), width)

                @pl.loop(0, (last - first) // block, unroll=2)
                def _(b):
                    at = pl.multiple_of(first + b * block, block)
                    total = jnp.zeros((block, HD), jnp.float32)
                    for _, start, ref in some:
                        x = load(ref, at, start)
                        for c in range(0, width, HD):
                            total = total + x[:, c : c + HD] * x[:, c : c + HD]
                    total = jnp.sum(total, -1, keepdims=True)
                    scale = lax.rsqrt(total * (1.0 / depth) + EPS)
                    for step, start, ref in some:
                        chunk = place_of(step)
                        encoded[pl.ds(at, block), chunk] = (
                            load(ref, at, start) * scale * gain_ref[:, chunk]
                        ).astype(jnp.bfloat16)

            refs_of = [(step, start, ref) for (step, start, _), ref in zip(parts, part_refs)]
            if parts[0][0] is None:
                refs_of = [((p,), 0, part_refs[0].at[p]) for p in range(size)]
            edges = sorted({0, rows} | {start for _, start, _ in refs_of})
            for first, last in zip(edges, edges[1:]):
                group(first, last, [r for r in refs_of if r[1] <= first and last <= r[1] + r[2].shape[0]])

        rows_now = encoded[...]
        key_out[...] = jnp.dot(rows_now, key_ref[...], preferred_element_type=jnp.float32).astype(jnp.bfloat16)
        value_out[...] = jnp.dot(rows_now, value_ref[...], preferred_element_type=jnp.float32).astype(jnp.bfloat16)

    out = jax.ShapeDtypeStruct((rows, columns), jnp.bfloat16)
    return pl.pallas_call(
        body,
        grid=(columns // tile,),
        out_shape=(out, out),
        in_specs=[
            pl.BlockSpec(memory_space=pltpu.SMEM),
            pl.BlockSpec((1, depth), lambda i: (0, 0)),
            pl.BlockSpec((depth, tile), lambda i: (0, i)),
            pl.BlockSpec((depth, tile), lambda i: (0, i)),
        ]
        + [pl.BlockSpec(x.shape, lambda i, n=x.ndim: (0,) * n) for _, _, x in parts],
        out_specs=(pl.BlockSpec((rows, tile), lambda i: (0, i)), pl.BlockSpec((rows, tile), lambda i: (0, i))),
        scratch_shapes=[pltpu.VMEM((rows, depth), jnp.bfloat16)],
        compiler_params=pltpu.CompilerParams(vmem_limit_bytes=KERNEL_VMEM),
        cost_estimate=pl.CostEstimate(
            flops=4 * rows * depth * columns, bytes_accessed=4 * depth * columns + 2 * rows * depth, transcendentals=0
        ),
        name="norm_and_project",
    )(here, gain.reshape(1, depth), key_matrix, value_matrix, *[x for _, _, x in parts])


def attend(queries, keys, values, counts):
    stretches = counts.shape[0]
    tokens, width = queries.shape
    stretch = tokens // stretches
    heads = width // HD
    spans = [k.shape[1] for k in keys]
    span = sum(spans)
    n = len(keys)

    per = 2

    def body(count_ref, query_ref, *refs):
        key_refs, value_refs, out_ref = refs[:n], refs[n : 2 * n], refs[2 * n]
        column = lax.broadcasted_iota(jnp.int32, (1, span), 1)
        neighbour = jnp.zeros((1, span), jnp.int32)
        start = 0
        for s in spans:
            for k in range(1, NBR):
                low = start + k * (s // NBR)
                neighbour = jnp.where((column >= low) & (column < low + s // NBR), k, neighbour)
            start += s
        at = [slice(h * HD, (h + 1) * HD) for h in range(heads)]
        for c in range(per):
            row = slice(c * stretch, (c + 1) * stretch)
            kept = neighbour < count_ref[pl.program_id(0) * per + c]
            scores = []
            for a in at:
                k = jnp.concatenate([r[c, :, a] for r in key_refs], 0)
                scores.append(
                    lax.dot_general(
                        query_ref[row, a], k, (((1,), (1,)), ((), ())), preferred_element_type=jnp.float32
                    )
                )
            scores = jnp.concatenate(scores, 0) * HD ** (-0.5)
            scores = jnp.where(kept, scores, -1e30)
            exponents = jnp.exp(scores - jnp.max(scores, -1, keepdims=True))
            weights = (exponents / jnp.sum(exponents, -1, keepdims=True)).astype(jnp.bfloat16)
            for h, a in enumerate(at):
                v = jnp.concatenate([r[c, :, a] for r in value_refs], 0)
                out_ref[row, a] = jnp.dot(
                    weights[h * stretch : (h + 1) * stretch], v, preferred_element_type=jnp.float32
                ).astype(jnp.bfloat16)

    return pl.pallas_call(
        body,
        grid=(stretches // per,),
        out_shape=jax.ShapeDtypeStruct(queries.shape, queries.dtype),
        in_specs=[pl.BlockSpec(memory_space=pltpu.SMEM), pl.BlockSpec((per * stretch, width), lambda c: (c, 0))]
        + [pl.BlockSpec((per, s, width), lambda c: (c, 0, 0)) for s in spans + spans],
        out_specs=pl.BlockSpec((per * stretch, width), lambda c: (c, 0)),
        compiler_params=pltpu.CompilerParams(vmem_limit_bytes=KERNEL_VMEM),
        cost_estimate=pl.CostEstimate(
            flops=4 * tokens * span * width, bytes_accessed=4 * (tokens + stretches * span) * width, transcendentals=tokens * span * heads
        ),
        name="attention",
    )(counts, queries, *keys, *values)


def per_device(queries, neighbours, norm_gain, key_weight, value_weight, slot_anchor, nbr_count):
    owners = lax.axis_size("section") * lax.axis_size("seq")
    slot_count = slot_anchor.shape[0]
    stretches = nbr_count.shape[0]
    width_part = neighbours.shape[1]
    capacity = 2 * ((slot_count // 2 + owners - 1) // owners)
    cells = owners * capacity

    source = slot_anchor // slot_count
    unit_index = slot_anchor % slot_count
    earlier = (source[None, :] == source[:, None]) & (slot_anchor[None, :] < slot_anchor[:, None])
    rank_among = jnp.sum(earlier.astype(jnp.int32), 1)
    grid_cell = source * capacity + rank_among
    cell_ids = jnp.arange(cells, dtype=jnp.int32)
    cell_match = grid_cell[None, :] == cell_ids[:, None]
    request = jnp.sum(jnp.where(cell_match, unit_index[None, :] + 1, 0), 1) - 1
    asked = lax.all_to_all(
        request.reshape(owners, capacity), OWN, split_axis=0, concat_axis=0, tiled=True
    ).reshape(cells)
    units = jnp.arange(slot_count, dtype=jnp.int32)
    position = jnp.max(jnp.where(asked[None, :] == units[:, None], cell_ids[None, :], 0), 1)

    pieces = neighbours.reshape(slot_count, PIECE, width_part)
    starts = [sum(CHUNKS[:j]) for j in range(len(CHUNKS))]
    count = len(CHUNKS)
    size = lax.axis_size("tp")

    def pick(j):
        return scatter_rows(position, pieces, starts[j], CHUNKS[j], cells).reshape(
            owners, capacity, CHUNKS[j], width_part
        )

    def place(j, arrived):
        return gather_rows(grid_cell, arrived.reshape(cells, CHUNKS[j], width_part)).reshape(-1, width_part)

    def shape_rows(x):
        return x.reshape(stretches, -1, x.shape[1])

    parts, done, halves = [], {}, {}

    def finish(j):
        done[j] = project(parts[j], norm_gain, key_weight[0], value_weight[0])

    picked = [pick(j) for j in range(count)]
    for j in range(count):
        ready = picked[j]
        if j >= 2:
            ready = after(ready, parts[j - 2][0][2])
        arrived = lax.all_to_all(ready, OWN, split_axis=0, concat_axis=0, tiled=True)
        if j == 0:
            arrived = after(arrived, *picked[1:])
        if j >= 3:
            finish(j - 3)
            arrived = after(arrived, done[j - 3][0])
        if j - 1 in halves:
            arrived = after(arrived, *halves[j - 1])
        own = place(j, arrived)
        if MODE[j] == "offload":
            full = lax.all_gather(own, "tp", axis=0)
            parts.append([(0, 0, own), (None, 0, full)])
            continue
        up, down = send(own, 1), send(own, size - 1)
        half = own.shape[0] // 2
        halves[j] = up[:half], down[half:]
        far = send(halves[j][0], 1), send(halves[j][1], size - 1)
        parts.append([(0, 0, own), (size - 1, 0, up), (1, 0, down), (2, 0, far[0]), (2, half, far[1])])
    parts[-2][-1] = parts[-2][-1][:2] + (after(parts[-2][-1][2], *halves[count - 1]),)
    parts[-3][-1] = parts[-3][-1][:2] + (after(parts[-3][-1][2], parts[-1][0][2]),)
    for j in range(count):
        if j not in done:
            finish(j)
    keys = [done[j][0] for j in range(count)]
    values = [done[j][1] for j in range(count)]
    keys = [shape_rows(x) for x in keys]
    values = [shape_rows(x) for x in values]
    return attend(queries, keys, values, nbr_count)


def solution(mesh):
    in_specs = (
        P(("section", "seq"), "tp"),
        P(("section", "seq"), "tp"),
        P(),
        P("section", None, "tp"),
        P("section", None, "tp"),
        P(("section", "seq")),
        P(("section", "seq")),
    )
    out_specs = P(("section", "seq"), "tp")
    return jax.shard_map(
        per_device, mesh=mesh, in_specs=in_specs, out_specs=out_specs, check_vma=False
    )
```

```python
import functools

import jax
import jax.numpy as jnp
from jax import lax
from jax.experimental import pallas as pl
from jax.experimental.pallas import tpu as pltpu
from jax.sharding import PartitionSpec as P

HD = 128
PIECE = 64
NBR = 2
CHUNKS = (16, 16, 16, 16)
MODE = ("offload", "ring", "offload", "ring")
EPS = 1e-05
OWN = ("section", "seq")
KERNEL_VMEM = 127 << 19


def scatter_rows(position, pieces, offset, rows, cells):
    count, _, width = pieces.shape

    def body(position_ref, pieces_ref, out_ref, held, sem, sems):
        load = pltpu.make_async_copy(pieces_ref.at[:, pl.ds(offset, rows)], held, sem)
        load.start()
        load.wait()

        def copy(u):
            return pltpu.make_async_copy(held.at[u], out_ref.at[position_ref[u]], sems.at[u])

        for u in range(count):
            copy(u).start()
        for u in range(count):
            copy(u).wait()

    return pl.pallas_call(
        body,
        out_shape=jax.ShapeDtypeStruct((cells, rows, width), pieces.dtype),
        in_specs=[pl.BlockSpec(memory_space=pltpu.SMEM), pl.BlockSpec(memory_space=pl.ANY)],
        out_specs=pl.BlockSpec(memory_space=pl.ANY),
        scratch_shapes=[
            pltpu.VMEM((count, rows, width), pieces.dtype),
            pltpu.SemaphoreType.DMA,
            pltpu.SemaphoreType.DMA((count,)),
        ],
        compiler_params=pltpu.CompilerParams(vmem_limit_bytes=KERNEL_VMEM),
        cost_estimate=pl.CostEstimate(flops=0, bytes_accessed=4 * count * rows * width, transcendentals=0),
        name="pick_rows",
    )(position, pieces)


def gather_rows(position, cells):
    count = position.shape[0]
    _, rows, width = cells.shape

    def body(position_ref, cells_ref, out_ref, held, sem, sems):
        def copy(t):
            return pltpu.make_async_copy(cells_ref.at[position_ref[t]], held.at[t], sems.at[t])

        for t in range(count):
            copy(t).start()
        for t in range(count):
            copy(t).wait()
        store = pltpu.make_async_copy(held, out_ref, sem)
        store.start()
        store.wait()

    return pl.pallas_call(
        body,
        out_shape=jax.ShapeDtypeStruct((count, rows, width), cells.dtype),
        in_specs=[pl.BlockSpec(memory_space=pltpu.SMEM), pl.BlockSpec(memory_space=pl.ANY)],
        out_specs=pl.BlockSpec(memory_space=pl.ANY),
        scratch_shapes=[
            pltpu.VMEM((count, rows, width), cells.dtype),
            pltpu.SemaphoreType.DMA,
            pltpu.SemaphoreType.DMA((count,)),
        ],
        compiler_params=pltpu.CompilerParams(vmem_limit_bytes=KERNEL_VMEM),
        cost_estimate=pl.CostEstimate(flops=0, bytes_accessed=4 * count * rows * width, transcendentals=0),
        name="place_rows",
    )(position, cells)


def after(x, *others):
    return lax.optimization_barrier((x,) + others)[0]


def send(x, step):
    size = lax.axis_size("tp")
    return lax.ppermute(x, "tp", [(i, (i + step) % size) for i in range(size)])


def project(parts, gain, key_matrix, value_matrix):
    if parts[-1][0] is None:
        parts = parts[1:]
    rows, width = parts[0][2].shape[-2:]
    depth, columns = key_matrix.shape
    size = depth // width
    tile = 256
    block = 16
    here = lax.axis_index("tp").astype(jnp.int32).reshape(1)
    n = len(parts)

    def body(here_ref, gain_ref, key_ref, value_ref, *refs):
        part_refs, key_out, value_out, encoded = refs[:n], refs[n], refs[n + 1], refs[n + 2]

        @pl.when(pl.program_id(0) == 0)
        def _():
            def group(first, last, some):
                def load(ref, at, start):
                    return ref[pl.ds(pl.multiple_of(at - start, block), block), :].astype(jnp.float32)

                def place_of(step):
                    if isinstance(step, tuple):
                        return slice(step[0] * width, (step[0] + 1) * width)
                    return pl.ds(pl.multiple_of((here_ref[0] + step) % size * width, width), width)

                @pl.loop(0, (last - first) // block, unroll=2)
                def _(b):
                    at = pl.multiple_of(first + b * block, block)
                    total = jnp.zeros((block, HD), jnp.float32)
                    for _, start, ref in some:
                        x = load(ref, at, start)
                        for c in range(0, width, HD):
                            total = total + x[:, c : c + HD] * x[:, c : c + HD]
                    total = jnp.sum(total, -1, keepdims=True)
                    scale = lax.rsqrt(total * (1.0 / depth) + EPS)
                    for step, start, ref in some:
                        chunk = place_of(step)
                        encoded[pl.ds(at, block), chunk] = (
                            load(ref, at, start) * scale * gain_ref[:, chunk]
                        ).astype(jnp.bfloat16)

            refs_of = [(step, start, ref) for (step, start, _), ref in zip(parts, part_refs)]
            if parts[0][0] is None:
                refs_of = [((p,), 0, part_refs[0].at[p]) for p in range(size)]
            edges = sorted({0, rows} | {start for _, start, _ in refs_of})
            for first, last in zip(edges, edges[1:]):
                group(first, last, [r for r in refs_of if r[1] <= first and last <= r[1] + r[2].shape[0]])

        rows_now = encoded[...]
        key_out[...] = jnp.dot(rows_now, key_ref[...], preferred_element_type=jnp.float32).astype(jnp.bfloat16)
        value_out[...] = jnp.dot(rows_now, value_ref[...], preferred_element_type=jnp.float32).astype(jnp.bfloat16)

    out = jax.ShapeDtypeStruct((rows, columns), jnp.bfloat16)
    return pl.pallas_call(
        body,
        grid=(columns // tile,),
        out_shape=(out, out),
        in_specs=[
            pl.BlockSpec(memory_space=pltpu.SMEM),
            pl.BlockSpec((1, depth), lambda i: (0, 0)),
            pl.BlockSpec((depth, tile), lambda i: (0, i)),
            pl.BlockSpec((depth, tile), lambda i: (0, i)),
        ]
        + [pl.BlockSpec(x.shape, lambda i, n=x.ndim: (0,) * n) for _, _, x in parts],
        out_specs=(pl.BlockSpec((rows, tile), lambda i: (0, i)), pl.BlockSpec((rows, tile), lambda i: (0, i))),
        scratch_shapes=[pltpu.VMEM((rows, depth), jnp.bfloat16)],
        compiler_params=pltpu.CompilerParams(vmem_limit_bytes=KERNEL_VMEM),
        cost_estimate=pl.CostEstimate(
            flops=4 * rows * depth * columns, bytes_accessed=4 * depth * columns + 2 * rows * depth, transcendentals=0
        ),
        name="norm_and_project",
    )(here, gain.reshape(1, depth), key_matrix, value_matrix, *[x for _, _, x in parts])


def project_parts(parts, scale, gain, key_matrix, value_matrix, sums=None):
    rows = scale.shape[0]
    width = parts[0][2].shape[1]
    depth, columns = key_matrix.shape
    size = depth // width
    tile = 256
    block = 16
    here = lax.axis_index("tp").astype(jnp.int32).reshape(1)
    steps = list(dict.fromkeys(step for step, _, _ in parts))
    n, m = len(parts), len(steps)

    def body(here_ref, scale_ref, *refs):
        gain_refs, key_refs, value_refs = refs[:m], refs[m : 2 * m], refs[2 * m : 3 * m]
        part_refs, refs = refs[3 * m : 3 * m + n], refs[3 * m + n :]
        sum_refs, (key_out, value_out, encoded) = refs[:-3], refs[-3:]

        @pl.when(pl.program_id(0) == 0)
        def _():
            for (step, start, _), ref in zip(parts, part_refs):
                p = steps.index(step)

                @pl.loop(0, ref.shape[0] // block, unroll=2)
                def _(b):
                    at = pl.multiple_of(b * block, block)
                    x = ref[pl.ds(at, block), :].astype(jnp.float32)
                    x = x * scale_ref[pl.ds(pl.multiple_of(start + at, block), block), :1] * gain_refs[p][...]
                    encoded[p, pl.ds(pl.multiple_of(start + at, block), block), :] = x.astype(jnp.bfloat16)

        key_sum = sum(jnp.dot(encoded[p], key_refs[p][...], preferred_element_type=jnp.float32) for p in range(m))
        value_sum = sum(jnp.dot(encoded[p], value_refs[p][...], preferred_element_type=jnp.float32) for p in range(m))
        if sum_refs:
            key_sum, value_sum = sum_refs[0][...] + key_sum, sum_refs[1][...] + value_sum
        key_out[...] = key_sum.astype(key_out.dtype)
        value_out[...] = value_sum.astype(value_out.dtype)

    sums = list(sums) if sums is not None else []
    column = pl.BlockSpec((rows, tile), lambda i, here: (0, i))
    matrix = [pl.BlockSpec((width, tile), lambda i, here, s=s: ((here[0] + s) % size, i)) for s in steps]
    out = jax.ShapeDtypeStruct((rows, columns), jnp.bfloat16 if sums else jnp.float32)
    return pl.pallas_call(
        body,
        grid_spec=pltpu.PrefetchScalarGridSpec(
            num_scalar_prefetch=1,
            grid=(columns // tile,),
            in_specs=[pl.BlockSpec(scale.shape, lambda i, here: (0, 0))]
            + [pl.BlockSpec((1, width), lambda i, here, s=s: (0, (here[0] + s) % size)) for s in steps]
            + matrix
            + matrix
            + [pl.BlockSpec(x.shape, lambda i, here: (0, 0)) for _, _, x in parts]
            + [column] * len(sums),
            out_specs=(column, column),
            scratch_shapes=[pltpu.VMEM((m, rows, width), jnp.bfloat16)],
        ),
        out_shape=(out, out),
        compiler_params=pltpu.CompilerParams(vmem_limit_bytes=KERNEL_VMEM),
        cost_estimate=pl.CostEstimate(
            flops=4 * rows * m * width * columns, bytes_accessed=4 * m * width * columns, transcendentals=0
        ),
        name="project_parts",
    )(
        here,
        scale,
        *[gain.reshape(1, depth)] * m,
        *[key_matrix] * m,
        *[value_matrix] * m,
        *[x for _, _, x in parts],
        *sums,
    )


def attend(queries, keys, values, counts):
    stretches = counts.shape[0]
    tokens, width = queries.shape
    stretch = tokens // stretches
    heads = width // HD
    spans = [k.shape[1] for k in keys]
    span = sum(spans)
    n = len(keys)

    per = 2

    def body(count_ref, query_ref, *refs):
        key_refs, value_refs, out_ref = refs[:n], refs[n : 2 * n], refs[2 * n]
        column = lax.broadcasted_iota(jnp.int32, (1, span), 1)
        neighbour = jnp.zeros((1, span), jnp.int32)
        start = 0
        for s in spans:
            for k in range(1, NBR):
                low = start + k * (s // NBR)
                neighbour = jnp.where((column >= low) & (column < low + s // NBR), k, neighbour)
            start += s
        at = [slice(h * HD, (h + 1) * HD) for h in range(heads)]
        for c in range(per):
            row = slice(c * stretch, (c + 1) * stretch)
            kept = neighbour < count_ref[pl.program_id(0) * per + c]
            scores = []
            for a in at:
                k = jnp.concatenate([r[c, :, a] for r in key_refs], 0)
                scores.append(
                    lax.dot_general(
                        query_ref[row, a], k, (((1,), (1,)), ((), ())), preferred_element_type=jnp.float32
                    )
                )
            scores = jnp.concatenate(scores, 0) * HD ** (-0.5)
            scores = jnp.where(kept, scores, -1e30)
            exponents = jnp.exp(scores - jnp.max(scores, -1, keepdims=True))
            weights = (exponents / jnp.sum(exponents, -1, keepdims=True)).astype(jnp.bfloat16)
            for h, a in enumerate(at):
                v = jnp.concatenate([r[c, :, a] for r in value_refs], 0)
                out_ref[row, a] = jnp.dot(
                    weights[h * stretch : (h + 1) * stretch], v, preferred_element_type=jnp.float32
                ).astype(jnp.bfloat16)

    return pl.pallas_call(
        body,
        grid=(stretches // per,),
        out_shape=jax.ShapeDtypeStruct(queries.shape, queries.dtype),
        in_specs=[pl.BlockSpec(memory_space=pltpu.SMEM), pl.BlockSpec((per * stretch, width), lambda c: (c, 0))]
        + [pl.BlockSpec((per, s, width), lambda c: (c, 0, 0)) for s in spans + spans],
        out_specs=pl.BlockSpec((per * stretch, width), lambda c: (c, 0)),
        compiler_params=pltpu.CompilerParams(vmem_limit_bytes=KERNEL_VMEM),
        cost_estimate=pl.CostEstimate(
            flops=4 * tokens * span * width, bytes_accessed=4 * (tokens + stretches * span) * width, transcendentals=tokens * span * heads
        ),
        name="attention",
    )(counts, queries, *keys, *values)


def per_device(queries, neighbours, norm_gain, key_weight, value_weight, slot_anchor, nbr_count):
    owners = lax.axis_size("section") * lax.axis_size("seq")
    slot_count = slot_anchor.shape[0]
    stretches = nbr_count.shape[0]
    width_part = neighbours.shape[1]
    capacity = 2 * ((slot_count // 2 + owners - 1) // owners)
    cells = owners * capacity

    source = slot_anchor // slot_count
    unit_index = slot_anchor % slot_count
    earlier = (source[None, :] == source[:, None]) & (slot_anchor[None, :] < slot_anchor[:, None])
    rank_among = jnp.sum(earlier.astype(jnp.int32), 1)
    grid_cell = source * capacity + rank_among
    cell_ids = jnp.arange(cells, dtype=jnp.int32)
    cell_match = grid_cell[None, :] == cell_ids[:, None]
    request = jnp.sum(jnp.where(cell_match, unit_index[None, :] + 1, 0), 1) - 1
    asked = lax.all_to_all(
        request.reshape(owners, capacity), OWN, split_axis=0, concat_axis=0, tiled=True
    ).reshape(cells)
    units = jnp.arange(slot_count, dtype=jnp.int32)
    position = jnp.max(jnp.where(asked[None, :] == units[:, None], cell_ids[None, :], 0), 1)

    pieces = neighbours.reshape(slot_count, PIECE, width_part)
    starts = [sum(CHUNKS[:j]) for j in range(len(CHUNKS))]
    count = len(CHUNKS)
    size = lax.axis_size("tp")

    def pick(j):
        return scatter_rows(position, pieces, starts[j], CHUNKS[j], cells).reshape(
            owners, capacity, CHUNKS[j], width_part
        )

    def place(j, arrived):
        return gather_rows(grid_cell, arrived.reshape(cells, CHUNKS[j], width_part)).reshape(-1, width_part)

    def shape_rows(x):
        return x.reshape(stretches, -1, x.shape[1])

    parts, done, halves = [], {}, {}

    def finish(j):
        done[j] = project(parts[j], norm_gain, key_weight[0], value_weight[0])

    picked = [pick(j) for j in range(count)]
    for j in range(count):
        ready = picked[j]
        if j >= 2:
            ready = after(ready, parts[j - 2][0][2])
        arrived = lax.all_to_all(ready, OWN, split_axis=0, concat_axis=0, tiled=True)
        if j == 0:
            arrived = after(arrived, *picked[1:])
        if j >= 3:
            finish(0)
            finish(1)
            arrived = after(arrived, done[0][0], done[1][0])
        if j - 1 in halves:
            arrived = after(arrived, *halves[j - 1])
        own = place(j, arrived)
        if MODE[j] == "offload":
            full = lax.all_gather(own, "tp", axis=0)
            parts.append([(0, 0, own), (None, 0, full)])
            continue
        up, down = send(own, 1), send(own, size - 1)
        half = own.shape[0] // 2
        halves[j] = up[:half], down[half:]
        far = send(halves[j][0], 1), send(halves[j][1], size - 1)
        parts.append([(0, 0, own), (size - 1, 0, up), (1, 0, down), (2, 0, far[0]), (2, half, far[1])])
    last = count - 1
    own = parts[last][0][2]
    squares = jnp.sum(jnp.square(own.astype(jnp.float32)), -1)
    squares = squares + send(squares, 1) + send(squares, 2) + send(squares, 3)
    scale = lax.rsqrt(squares * (1.0 / (size * width_part)) + EPS)
    scale = jnp.broadcast_to(scale[:, None], (scale.shape[0], HD))
    for j in range(last):
        if j not in done:
            parts[j][-1] = parts[j][-1][:2] + (after(parts[j][-1][2], own),)
            finish(j)
    halves[last] = lax.optimization_barrier((*halves[last], *[done[j][0] for j in range(last)]))[:2]
    matrices = norm_gain, key_weight[0], value_weight[0]
    parts[last][3:] = [(2, 0, send(halves[last][0], 1)), (2, own.shape[0] // 2, send(halves[last][1], size - 1))]
    sums = project_parts(parts[last][:3], after(scale, *halves[last]), *matrices)
    done[last] = project_parts(parts[last][3:], scale, *matrices, sums=sums)
    keys = [done[j][0] for j in range(count)]
    values = [done[j][1] for j in range(count)]
    keys = [shape_rows(x) for x in keys]
    values = [shape_rows(x) for x in values]
    return attend(queries, keys, values, nbr_count)


def solution(mesh):
    in_specs = (
        P(("section", "seq"), "tp"),
        P(("section", "seq"), "tp"),
        P(),
        P("section", None, "tp"),
        P("section", None, "tp"),
        P(("section", "seq")),
        P(("section", "seq")),
    )
    out_specs = P(("section", "seq"), "tp")
    return jax.shard_map(
        per_device, mesh=mesh, in_specs=in_specs, out_specs=out_specs, check_vma=False
    )
```

```python
import functools

import jax
import jax.numpy as jnp
from jax import lax
from jax.experimental import pallas as pl
from jax.experimental.pallas import tpu as pltpu
from jax.sharding import PartitionSpec as P

HD = 128
PIECE = 64
NBR = 2
CHUNKS = (32, 16, 16)
MODE = ("offload", "ring", "ring")
EPS = 1e-05
OWN = ("section", "seq")
KERNEL_VMEM = 127 << 19


def scatter_rows(position, pieces, offset, rows, cells):
    count, _, width = pieces.shape

    def body(position_ref, pieces_ref, out_ref, held, sem, sems):
        load = pltpu.make_async_copy(pieces_ref.at[:, pl.ds(offset, rows)], held, sem)
        load.start()
        load.wait()

        def copy(u):
            return pltpu.make_async_copy(held.at[u], out_ref.at[position_ref[u]], sems.at[u])

        for u in range(count):
            copy(u).start()
        for u in range(count):
            copy(u).wait()

    return pl.pallas_call(
        body,
        out_shape=jax.ShapeDtypeStruct((cells, rows, width), pieces.dtype),
        in_specs=[pl.BlockSpec(memory_space=pltpu.SMEM), pl.BlockSpec(memory_space=pl.ANY)],
        out_specs=pl.BlockSpec(memory_space=pl.ANY),
        scratch_shapes=[
            pltpu.VMEM((count, rows, width), pieces.dtype),
            pltpu.SemaphoreType.DMA,
            pltpu.SemaphoreType.DMA((count,)),
        ],
        compiler_params=pltpu.CompilerParams(vmem_limit_bytes=KERNEL_VMEM),
        cost_estimate=pl.CostEstimate(flops=0, bytes_accessed=4 * count * rows * width, transcendentals=0),
        name="pick_rows",
    )(position, pieces)


def gather_rows(position, cells):
    count = position.shape[0]
    _, rows, width = cells.shape

    def body(position_ref, cells_ref, out_ref, held, sem, sems):
        def copy(t):
            return pltpu.make_async_copy(cells_ref.at[position_ref[t]], held.at[t], sems.at[t])

        for t in range(count):
            copy(t).start()
        for t in range(count):
            copy(t).wait()
        store = pltpu.make_async_copy(held, out_ref, sem)
        store.start()
        store.wait()

    return pl.pallas_call(
        body,
        out_shape=jax.ShapeDtypeStruct((count, rows, width), cells.dtype),
        in_specs=[pl.BlockSpec(memory_space=pltpu.SMEM), pl.BlockSpec(memory_space=pl.ANY)],
        out_specs=pl.BlockSpec(memory_space=pl.ANY),
        scratch_shapes=[
            pltpu.VMEM((count, rows, width), cells.dtype),
            pltpu.SemaphoreType.DMA,
            pltpu.SemaphoreType.DMA((count,)),
        ],
        compiler_params=pltpu.CompilerParams(vmem_limit_bytes=KERNEL_VMEM),
        cost_estimate=pl.CostEstimate(flops=0, bytes_accessed=4 * count * rows * width, transcendentals=0),
        name="place_rows",
    )(position, cells)


def after(x, *others):
    return lax.optimization_barrier((x,) + others)[0]


def send(x, step):
    size = lax.axis_size("tp")
    return lax.ppermute(x, "tp", [(i, (i + step) % size) for i in range(size)])


def project(parts, gain, key_matrix, value_matrix):
    if parts[-1][0] is None:
        parts = parts[1:]
    rows, width = parts[0][2].shape[-2:]
    depth, columns = key_matrix.shape
    size = depth // width
    tile = 256
    block = 16
    here = lax.axis_index("tp").astype(jnp.int32).reshape(1)
    n = len(parts)

    def body(here_ref, gain_ref, key_ref, value_ref, *refs):
        part_refs, key_out, value_out, encoded = refs[:n], refs[n], refs[n + 1], refs[n + 2]

        @pl.when(pl.program_id(0) == 0)
        def _():
            def group(first, last, some):
                def load(ref, at, start):
                    return ref[pl.ds(pl.multiple_of(at - start, block), block), :].astype(jnp.float32)

                def place_of(step):
                    if isinstance(step, tuple):
                        return slice(step[0] * width, (step[0] + 1) * width)
                    return pl.ds(pl.multiple_of((here_ref[0] + step) % size * width, width), width)

                @pl.loop(0, (last - first) // block, unroll=2)
                def _(b):
                    at = pl.multiple_of(first + b * block, block)
                    total = jnp.zeros((block, HD), jnp.float32)
                    for _, start, ref in some:
                        x = load(ref, at, start)
                        for c in range(0, width, HD):
                            total = total + x[:, c : c + HD] * x[:, c : c + HD]
                    total = jnp.sum(total, -1, keepdims=True)
                    scale = lax.rsqrt(total * (1.0 / depth) + EPS)
                    for step, start, ref in some:
                        chunk = place_of(step)
                        encoded[pl.ds(at, block), chunk] = (
                            load(ref, at, start) * scale * gain_ref[:, chunk]
                        ).astype(jnp.bfloat16)

            refs_of = [(step, start, ref) for (step, start, _), ref in zip(parts, part_refs)]
            if parts[0][0] is None:
                refs_of = [((p,), 0, part_refs[0].at[p]) for p in range(size)]
            edges = sorted({0, rows} | {start for _, start, _ in refs_of})
            for first, last in zip(edges, edges[1:]):
                group(first, last, [r for r in refs_of if r[1] <= first and last <= r[1] + r[2].shape[0]])

        rows_now = encoded[...]
        key_out[...] = jnp.dot(rows_now, key_ref[...], preferred_element_type=jnp.float32).astype(jnp.bfloat16)
        value_out[...] = jnp.dot(rows_now, value_ref[...], preferred_element_type=jnp.float32).astype(jnp.bfloat16)

    out = jax.ShapeDtypeStruct((rows, columns), jnp.bfloat16)
    return pl.pallas_call(
        body,
        grid=(columns // tile,),
        out_shape=(out, out),
        in_specs=[
            pl.BlockSpec(memory_space=pltpu.SMEM),
            pl.BlockSpec((1, depth), lambda i: (0, 0)),
            pl.BlockSpec((depth, tile), lambda i: (0, i)),
            pl.BlockSpec((depth, tile), lambda i: (0, i)),
        ]
        + [pl.BlockSpec(x.shape, lambda i, n=x.ndim: (0,) * n) for _, _, x in parts],
        out_specs=(pl.BlockSpec((rows, tile), lambda i: (0, i)), pl.BlockSpec((rows, tile), lambda i: (0, i))),
        scratch_shapes=[pltpu.VMEM((rows, depth), jnp.bfloat16)],
        compiler_params=pltpu.CompilerParams(vmem_limit_bytes=KERNEL_VMEM),
        cost_estimate=pl.CostEstimate(
            flops=4 * rows * depth * columns, bytes_accessed=4 * depth * columns + 2 * rows * depth, transcendentals=0
        ),
        name="norm_and_project",
    )(here, gain.reshape(1, depth), key_matrix, value_matrix, *[x for _, _, x in parts])


def attend(queries, keys, values, counts):
    stretches = counts.shape[0]
    tokens, width = queries.shape
    stretch = tokens // stretches
    heads = width // HD
    spans = [k.shape[1] for k in keys]
    span = sum(spans)
    n = len(keys)

    per = 2

    def body(count_ref, query_ref, *refs):
        key_refs, value_refs, out_ref = refs[:n], refs[n : 2 * n], refs[2 * n]
        column = lax.broadcasted_iota(jnp.int32, (1, span), 1)
        neighbour = jnp.zeros((1, span), jnp.int32)
        start = 0
        for s in spans:
            for k in range(1, NBR):
                low = start + k * (s // NBR)
                neighbour = jnp.where((column >= low) & (column < low + s // NBR), k, neighbour)
            start += s
        at = [slice(h * HD, (h + 1) * HD) for h in range(heads)]
        for c in range(per):
            row = slice(c * stretch, (c + 1) * stretch)
            kept = neighbour < count_ref[pl.program_id(0) * per + c]
            scores = []
            for a in at:
                k = jnp.concatenate([r[c, :, a] for r in key_refs], 0)
                scores.append(
                    lax.dot_general(
                        query_ref[row, a], k, (((1,), (1,)), ((), ())), preferred_element_type=jnp.float32
                    )
                )
            scores = jnp.concatenate(scores, 0) * HD ** (-0.5)
            scores = jnp.where(kept, scores, -1e30)
            exponents = jnp.exp(scores - jnp.max(scores, -1, keepdims=True))
            weights = (exponents / jnp.sum(exponents, -1, keepdims=True)).astype(jnp.bfloat16)
            for h, a in enumerate(at):
                v = jnp.concatenate([r[c, :, a] for r in value_refs], 0)
                out_ref[row, a] = jnp.dot(
                    weights[h * stretch : (h + 1) * stretch], v, preferred_element_type=jnp.float32
                ).astype(jnp.bfloat16)

    return pl.pallas_call(
        body,
        grid=(stretches // per,),
        out_shape=jax.ShapeDtypeStruct(queries.shape, queries.dtype),
        in_specs=[pl.BlockSpec(memory_space=pltpu.SMEM), pl.BlockSpec((per * stretch, width), lambda c: (c, 0))]
        + [pl.BlockSpec((per, s, width), lambda c: (c, 0, 0)) for s in spans + spans],
        out_specs=pl.BlockSpec((per * stretch, width), lambda c: (c, 0)),
        compiler_params=pltpu.CompilerParams(vmem_limit_bytes=KERNEL_VMEM),
        cost_estimate=pl.CostEstimate(
            flops=4 * tokens * span * width, bytes_accessed=4 * (tokens + stretches * span) * width, transcendentals=tokens * span * heads
        ),
        name="attention",
    )(counts, queries, *keys, *values)


def per_device(queries, neighbours, norm_gain, key_weight, value_weight, slot_anchor, nbr_count):
    owners = lax.axis_size("section") * lax.axis_size("seq")
    slot_count = slot_anchor.shape[0]
    stretches = nbr_count.shape[0]
    width_part = neighbours.shape[1]
    capacity = 2 * ((slot_count // 2 + owners - 1) // owners)
    cells = owners * capacity

    source = slot_anchor // slot_count
    unit_index = slot_anchor % slot_count
    earlier = (source[None, :] == source[:, None]) & (slot_anchor[None, :] < slot_anchor[:, None])
    rank_among = jnp.sum(earlier.astype(jnp.int32), 1)
    grid_cell = source * capacity + rank_among
    cell_ids = jnp.arange(cells, dtype=jnp.int32)
    cell_match = grid_cell[None, :] == cell_ids[:, None]
    request = jnp.sum(jnp.where(cell_match, unit_index[None, :] + 1, 0), 1) - 1
    asked = lax.all_to_all(
        request.reshape(owners, capacity), OWN, split_axis=0, concat_axis=0, tiled=True
    ).reshape(cells)
    units = jnp.arange(slot_count, dtype=jnp.int32)
    position = jnp.max(jnp.where(asked[None, :] == units[:, None], cell_ids[None, :], 0), 1)

    pieces = neighbours.reshape(slot_count, PIECE, width_part)
    starts = [sum(CHUNKS[:j]) for j in range(len(CHUNKS))]
    count = len(CHUNKS)
    size = lax.axis_size("tp")

    def pick(j):
        return scatter_rows(position, pieces, starts[j], CHUNKS[j], cells).reshape(
            owners, capacity, CHUNKS[j], width_part
        )

    def place(j, arrived):
        return gather_rows(grid_cell, arrived.reshape(cells, CHUNKS[j], width_part)).reshape(-1, width_part)

    def shape_rows(x):
        return x.reshape(stretches, -1, x.shape[1])

    parts, done, halves = [], {}, {}

    def finish(j):
        done[j] = project(parts[j], norm_gain, key_weight[0], value_weight[0])

    picked = [pick(j) for j in range(count)]
    for j in range(count):
        ready = picked[j]
        if j >= 2:
            ready = after(ready, parts[j - 2][0][2])
        arrived = lax.all_to_all(ready, OWN, split_axis=0, concat_axis=0, tiled=True)
        if j == 0:
            arrived = after(arrived, *picked[1:])
        if j >= 3:
            finish(j - 3)
            arrived = after(arrived, done[j - 3][0])
        if j - 1 in halves:
            arrived = after(arrived, *halves[j - 1])
        own = place(j, arrived)
        if MODE[j] == "offload":
            full = lax.all_gather(own, "tp", axis=0)
            parts.append([(0, 0, own), (None, 0, full)])
            continue
        up, down = send(own, 1), send(own, size - 1)
        if j == count - 1:
            parts[0][-1] = parts[0][-1][:2] + (after(parts[0][-1][2], own),)
            finish(0)
            up, down = lax.optimization_barrier((up, down, done[0][0]))[:2]
        half = own.shape[0] // 2
        halves[j] = up[:half], down[half:]
        far = send(halves[j][0], 1), send(halves[j][1], size - 1)
        parts.append([(0, 0, own), (size - 1, 0, up), (1, 0, down), (2, 0, far[0]), (2, half, far[1])])
    parts[-2][-1] = parts[-2][-1][:2] + (after(parts[-2][-1][2], *halves[count - 1]),)
    for j in range(count):
        if j not in done:
            finish(j)
    keys = [done[j][0] for j in range(count)]
    values = [done[j][1] for j in range(count)]
    keys = [shape_rows(x) for x in keys]
    values = [shape_rows(x) for x in values]
    return attend(queries, keys, values, nbr_count)


def solution(mesh):
    in_specs = (
        P(("section", "seq"), "tp"),
        P(("section", "seq"), "tp"),
        P(),
        P("section", None, "tp"),
        P("section", None, "tp"),
        P(("section", "seq")),
        P(("section", "seq")),
    )
    out_specs = P(("section", "seq"), "tp")
    return jax.shard_map(
        per_device, mesh=mesh, in_specs=in_specs, out_specs=out_specs, check_vma=False
    )
```

```python
import functools

import jax
import jax.numpy as jnp
from jax import lax
from jax.experimental import pallas as pl
from jax.experimental.pallas import tpu as pltpu
from jax.sharding import PartitionSpec as P

HD = 128
PIECE = 64
NBR = 2
CHUNKS = (16, 16, 16, 16)
MODE = ("offload", "offload", "ring", "ring")
EPS = 1e-05
OWN = ("section", "seq")
KERNEL_VMEM = 127 << 19


def scatter_rows(position, pieces, offset, rows, cells):
    count, _, width = pieces.shape

    def body(position_ref, pieces_ref, out_ref, held, sem, sems):
        load = pltpu.make_async_copy(pieces_ref.at[:, pl.ds(offset, rows)], held, sem)
        load.start()
        load.wait()

        def copy(u):
            return pltpu.make_async_copy(held.at[u], out_ref.at[position_ref[u]], sems.at[u])

        for u in range(count):
            copy(u).start()
        for u in range(count):
            copy(u).wait()

    return pl.pallas_call(
        body,
        out_shape=jax.ShapeDtypeStruct((cells, rows, width), pieces.dtype),
        in_specs=[pl.BlockSpec(memory_space=pltpu.SMEM), pl.BlockSpec(memory_space=pl.ANY)],
        out_specs=pl.BlockSpec(memory_space=pl.ANY),
        scratch_shapes=[
            pltpu.VMEM((count, rows, width), pieces.dtype),
            pltpu.SemaphoreType.DMA,
            pltpu.SemaphoreType.DMA((count,)),
        ],
        compiler_params=pltpu.CompilerParams(vmem_limit_bytes=KERNEL_VMEM),
        cost_estimate=pl.CostEstimate(flops=0, bytes_accessed=4 * count * rows * width, transcendentals=0),
        name="pick_rows",
    )(position, pieces)


def gather_rows(position, cells):
    count = position.shape[0]
    _, rows, width = cells.shape

    def body(position_ref, cells_ref, out_ref, held, stored, sems):
        def copy(t):
            return pltpu.make_async_copy(cells_ref.at[position_ref[t]], held.at[t], sems.at[t])

        for t in range(count):
            copy(t).start()
        def store(t):
            return pltpu.make_async_copy(held.at[t], out_ref.at[t], stored.at[t])

        for t in range(count):
            copy(t).wait()
            store(t).start()
        for t in range(count):
            store(t).wait()

    return pl.pallas_call(
        body,
        out_shape=jax.ShapeDtypeStruct((count, rows, width), cells.dtype),
        in_specs=[pl.BlockSpec(memory_space=pltpu.SMEM), pl.BlockSpec(memory_space=pl.ANY)],
        out_specs=pl.BlockSpec(memory_space=pl.ANY),
        scratch_shapes=[
            pltpu.VMEM((count, rows, width), cells.dtype),
            pltpu.SemaphoreType.DMA((count,)),
            pltpu.SemaphoreType.DMA((count,)),
        ],
        compiler_params=pltpu.CompilerParams(vmem_limit_bytes=KERNEL_VMEM),
        cost_estimate=pl.CostEstimate(flops=0, bytes_accessed=4 * count * rows * width, transcendentals=0),
        name="place_rows",
    )(position, cells)


def after(x, *others):
    return lax.optimization_barrier((x,) + others)[0]


def send(x, step):
    size = lax.axis_size("tp")
    return lax.ppermute(x, "tp", [(i, (i + step) % size) for i in range(size)])


def project(parts, gain, key_matrix, value_matrix):
    if parts[-1][0] is None:
        parts = parts[1:]
    rows, width = parts[0][2].shape[-2:]
    depth, columns = key_matrix.shape
    size = depth // width
    tile = 256
    block = 16
    here = lax.axis_index("tp").astype(jnp.int32).reshape(1)
    n = len(parts)

    def body(here_ref, gain_ref, key_ref, value_ref, *refs):
        part_refs, key_out, value_out, encoded = refs[:n], refs[n], refs[n + 1], refs[n + 2]

        @pl.when(pl.program_id(0) == 0)
        def _():
            def group(first, last, some):
                def load(ref, at, start):
                    return ref[pl.ds(pl.multiple_of(at - start, block), block), :].astype(jnp.float32)

                def place_of(step):
                    if isinstance(step, tuple):
                        return slice(step[0] * width, (step[0] + 1) * width)
                    return pl.ds(pl.multiple_of((here_ref[0] + step) % size * width, width), width)

                @pl.loop(0, (last - first) // block, unroll=4)
                def _(b):
                    at = pl.multiple_of(first + b * block, block)
                    total = jnp.zeros((block, HD), jnp.float32)
                    for _, start, ref in some:
                        x = load(ref, at, start)
                        for c in range(0, width, HD):
                            total = total + x[:, c : c + HD] * x[:, c : c + HD]
                    total = jnp.sum(total, -1, keepdims=True)
                    scale = lax.rsqrt(total * (1.0 / depth) + EPS)
                    for step, start, ref in some:
                        chunk = place_of(step)
                        encoded[pl.ds(at, block), chunk] = (
                            load(ref, at, start) * scale * gain_ref[:, chunk]
                        ).astype(jnp.bfloat16)

            refs_of = [(step, start, ref) for (step, start, _), ref in zip(parts, part_refs)]
            if parts[0][0] is None:
                refs_of = [((p,), 0, part_refs[0].at[p]) for p in range(size)]
            edges = sorted({0, rows} | {start for _, start, _ in refs_of})
            for first, last in zip(edges, edges[1:]):
                group(first, last, [r for r in refs_of if r[1] <= first and last <= r[1] + r[2].shape[0]])

        rows_now = encoded[...]
        key_out[...] = jnp.dot(rows_now, key_ref[...], preferred_element_type=jnp.float32).astype(jnp.bfloat16)
        value_out[...] = jnp.dot(rows_now, value_ref[...], preferred_element_type=jnp.float32).astype(jnp.bfloat16)

    out = jax.ShapeDtypeStruct((rows, columns), jnp.bfloat16)
    return pl.pallas_call(
        body,
        grid=(columns // tile,),
        out_shape=(out, out),
        in_specs=[
            pl.BlockSpec(memory_space=pltpu.SMEM),
            pl.BlockSpec((1, depth), lambda i: (0, 0)),
            pl.BlockSpec((depth, tile), lambda i: (0, i)),
            pl.BlockSpec((depth, tile), lambda i: (0, i)),
        ]
        + [pl.BlockSpec(x.shape, lambda i, n=x.ndim: (0,) * n) for _, _, x in parts],
        out_specs=(pl.BlockSpec((rows, tile), lambda i: (0, i)), pl.BlockSpec((rows, tile), lambda i: (0, i))),
        scratch_shapes=[pltpu.VMEM((rows, depth), jnp.bfloat16)],
        compiler_params=pltpu.CompilerParams(vmem_limit_bytes=KERNEL_VMEM),
        cost_estimate=pl.CostEstimate(
            flops=4 * rows * depth * columns, bytes_accessed=4 * depth * columns + 2 * rows * depth, transcendentals=0
        ),
        name="norm_and_project",
    )(here, gain.reshape(1, depth), key_matrix, value_matrix, *[x for _, _, x in parts])


def attend(queries, keys, values, counts):
    stretches = counts.shape[0]
    tokens, width = queries.shape
    stretch = tokens // stretches
    heads = width // HD
    spans = [k.shape[1] for k in keys]
    span = sum(spans)
    n = len(keys)

    per = 2

    def body(count_ref, query_ref, *refs):
        key_refs, value_refs, out_ref = refs[:n], refs[n : 2 * n], refs[2 * n]
        column = lax.broadcasted_iota(jnp.int32, (1, span), 1)
        neighbour = jnp.zeros((1, span), jnp.int32)
        start = 0
        for s in spans:
            for k in range(1, NBR):
                low = start + k * (s // NBR)
                neighbour = jnp.where((column >= low) & (column < low + s // NBR), k, neighbour)
            start += s
        at = [slice(h * HD, (h + 1) * HD) for h in range(heads)]
        for c in range(per):
            row = slice(c * stretch, (c + 1) * stretch)
            kept = neighbour < count_ref[pl.program_id(0) * per + c]
            scores = []
            for a in at:
                k = jnp.concatenate([r[c, :, a] for r in key_refs], 0)
                scores.append(
                    lax.dot_general(
                        query_ref[row, a], k, (((1,), (1,)), ((), ())), preferred_element_type=jnp.float32
                    )
                )
            scores = jnp.concatenate(scores, 0) * HD ** (-0.5)
            scores = jnp.where(kept, scores, -1e30)
            exponents = jnp.exp(scores - jnp.max(scores, -1, keepdims=True))
            weights = (exponents / jnp.sum(exponents, -1, keepdims=True)).astype(jnp.bfloat16)
            for h, a in enumerate(at):
                v = jnp.concatenate([r[c, :, a] for r in value_refs], 0)
                out_ref[row, a] = jnp.dot(
                    weights[h * stretch : (h + 1) * stretch], v, preferred_element_type=jnp.float32
                ).astype(jnp.bfloat16)

    return pl.pallas_call(
        body,
        grid=(stretches // per,),
        out_shape=jax.ShapeDtypeStruct(queries.shape, queries.dtype),
        in_specs=[pl.BlockSpec(memory_space=pltpu.SMEM), pl.BlockSpec((per * stretch, width), lambda c: (c, 0))]
        + [pl.BlockSpec((per, s, width), lambda c: (c, 0, 0)) for s in spans + spans],
        out_specs=pl.BlockSpec((per * stretch, width), lambda c: (c, 0)),
        compiler_params=pltpu.CompilerParams(vmem_limit_bytes=KERNEL_VMEM),
        cost_estimate=pl.CostEstimate(
            flops=4 * tokens * span * width, bytes_accessed=4 * (tokens + stretches * span) * width, transcendentals=tokens * span * heads
        ),
        name="attention",
    )(counts, queries, *keys, *values)


def per_device(queries, neighbours, norm_gain, key_weight, value_weight, slot_anchor, nbr_count):
    owners = lax.axis_size("section") * lax.axis_size("seq")
    slot_count = slot_anchor.shape[0]
    stretches = nbr_count.shape[0]
    width_part = neighbours.shape[1]
    capacity = 2 * ((slot_count // 2 + owners - 1) // owners)
    cells = owners * capacity

    source = slot_anchor // slot_count
    unit_index = slot_anchor % slot_count
    earlier = (source[None, :] == source[:, None]) & (slot_anchor[None, :] < slot_anchor[:, None])
    rank_among = jnp.sum(earlier.astype(jnp.int32), 1)
    grid_cell = source * capacity + rank_among
    cell_ids = jnp.arange(cells, dtype=jnp.int32)
    cell_match = grid_cell[None, :] == cell_ids[:, None]
    request = jnp.sum(jnp.where(cell_match, unit_index[None, :] + 1, 0), 1) - 1
    asked = lax.all_to_all(
        request.reshape(owners, capacity), OWN, split_axis=0, concat_axis=0, tiled=True
    ).reshape(cells)
    units = jnp.arange(slot_count, dtype=jnp.int32)
    position = jnp.max(jnp.where(asked[None, :] == units[:, None], cell_ids[None, :], 0), 1)

    pieces = neighbours.reshape(slot_count, PIECE, width_part)
    starts = [sum(CHUNKS[:j]) for j in range(len(CHUNKS))]
    count = len(CHUNKS)
    size = lax.axis_size("tp")

    def pick(j):
        return scatter_rows(position, pieces, starts[j], CHUNKS[j], cells).reshape(
            owners, capacity, CHUNKS[j], width_part
        )

    def place(j, arrived):
        return gather_rows(grid_cell, arrived.reshape(cells, CHUNKS[j], width_part)).reshape(-1, width_part)

    def shape_rows(x):
        return x.reshape(stretches, -1, x.shape[1])

    parts, done, halves = [], {}, {}

    def finish(j):
        done[j] = project(parts[j], norm_gain, key_weight[0], value_weight[0])

    picked = [pick(j) for j in range(count)]
    for j in range(count):
        ready = picked[j]
        if j >= 2:
            ready = after(ready, parts[j - 2][0][2])
        if j == 3:
            finish(0)
            ready = after(ready, done[0][0])
        arrived = lax.all_to_all(ready, OWN, split_axis=0, concat_axis=0, tiled=True)
        if j == 0:
            arrived = after(arrived, *picked[1:])
        if j - 1 in halves:
            arrived = after(arrived, *halves[j - 1])
        own = place(j, arrived)
        if MODE[j] == "offload":
            full = lax.all_gather(own, "tp", axis=0)
            parts.append([(0, 0, own), (None, 0, full)])
            continue
        up, down = send(own, 1), send(own, size - 1)
        if j >= 2:
            parts[j - 1][-1] = parts[j - 1][-1][:2] + (after(parts[j - 1][-1][2], own),)
            finish(j - 1)
            up, down = lax.optimization_barrier((up, down, done[j - 1][0]))[:2]
        half = own.shape[0] // 2
        halves[j] = up[:half], down[half:]
        far = send(halves[j][0], 1), send(halves[j][1], size - 1)
        parts.append([(0, 0, own), (size - 1, 0, up), (1, 0, down), (2, 0, far[0]), (2, half, far[1])])
    for j in range(count):
        if j not in done:
            finish(j)
    keys = [done[j][0] for j in range(count)]
    values = [done[j][1] for j in range(count)]
    keys = [shape_rows(x) for x in keys]
    values = [shape_rows(x) for x in values]
    return attend(queries, keys, values, nbr_count)


def solution(mesh):
    in_specs = (
        P(("section", "seq"), "tp"),
        P(("section", "seq"), "tp"),
        P(),
        P("section", None, "tp"),
        P("section", None, "tp"),
        P(("section", "seq")),
        P(("section", "seq")),
    )
    out_specs = P(("section", "seq"), "tp")
    return jax.shard_map(
        per_device, mesh=mesh, in_specs=in_specs, out_specs=out_specs, check_vma=False
    )
```

```python
import functools

import jax
import jax.numpy as jnp
from jax import lax
from jax.experimental import pallas as pl
from jax.experimental.pallas import tpu as pltpu
from jax.sharding import PartitionSpec as P

HD = 128
PIECE = 64
NBR = 2
CHUNKS = (16, 16, 16, 16)
MODE = ("offload", "offload", "ring", "ring")
EPS = 1e-05
OWN = ("section", "seq")
KERNEL_VMEM = 127 << 19


def scatter_rows(position, pieces, offset, rows, cells):
    count, _, width = pieces.shape

    def body(position_ref, pieces_ref, out_ref, held, sem, sems):
        load = pltpu.make_async_copy(pieces_ref.at[:, pl.ds(offset, rows)], held, sem)
        load.start()
        load.wait()

        def copy(u):
            return pltpu.make_async_copy(held.at[u], out_ref.at[position_ref[u]], sems.at[u])

        for u in range(count):
            copy(u).start()
        for u in range(count):
            copy(u).wait()

    return pl.pallas_call(
        body,
        out_shape=jax.ShapeDtypeStruct((cells, rows, width), pieces.dtype),
        in_specs=[pl.BlockSpec(memory_space=pltpu.SMEM), pl.BlockSpec(memory_space=pl.ANY)],
        out_specs=pl.BlockSpec(memory_space=pl.ANY),
        scratch_shapes=[
            pltpu.VMEM((count, rows, width), pieces.dtype),
            pltpu.SemaphoreType.DMA,
            pltpu.SemaphoreType.DMA((count,)),
        ],
        compiler_params=pltpu.CompilerParams(vmem_limit_bytes=KERNEL_VMEM),
        cost_estimate=pl.CostEstimate(flops=0, bytes_accessed=4 * count * rows * width, transcendentals=0),
        name="pick_rows",
    )(position, pieces)


def gather_rows(position, cells):
    count = position.shape[0]
    _, rows, width = cells.shape

    def body(position_ref, cells_ref, out_ref, held, stored, sems):
        def copy(t):
            return pltpu.make_async_copy(cells_ref.at[position_ref[t]], held.at[t], sems.at[t])

        for t in range(count):
            copy(t).start()
        def store(t):
            return pltpu.make_async_copy(held.at[t], out_ref.at[t], stored.at[t])

        for t in range(count):
            copy(t).wait()
            store(t).start()
        for t in range(count):
            store(t).wait()

    return pl.pallas_call(
        body,
        out_shape=jax.ShapeDtypeStruct((count, rows, width), cells.dtype),
        in_specs=[pl.BlockSpec(memory_space=pltpu.SMEM), pl.BlockSpec(memory_space=pl.ANY)],
        out_specs=pl.BlockSpec(memory_space=pl.ANY),
        scratch_shapes=[
            pltpu.VMEM((count, rows, width), cells.dtype),
            pltpu.SemaphoreType.DMA((count,)),
            pltpu.SemaphoreType.DMA((count,)),
        ],
        compiler_params=pltpu.CompilerParams(vmem_limit_bytes=KERNEL_VMEM),
        cost_estimate=pl.CostEstimate(flops=0, bytes_accessed=4 * count * rows * width, transcendentals=0),
        name="place_rows",
    )(position, cells)


def after(x, *others):
    return lax.optimization_barrier((x,) + others)[0]


def send(x, step):
    size = lax.axis_size("tp")
    return lax.ppermute(x, "tp", [(i, (i + step) % size) for i in range(size)])


def project(parts, gain, key_matrix, value_matrix):
    if parts[-1][0] is None:
        parts = parts[1:]
    rows, width = parts[0][2].shape[-2:]
    depth, columns = key_matrix.shape
    size = depth // width
    tile = 256
    block = 16
    here = lax.axis_index("tp").astype(jnp.int32).reshape(1)
    n = len(parts)

    def body(here_ref, gain_ref, key_ref, value_ref, *refs):
        part_refs, key_out, value_out, encoded = refs[:n], refs[n], refs[n + 1], refs[n + 2]

        @pl.when(pl.program_id(0) == 0)
        def _():
            def group(first, last, some):
                def load(ref, at, start):
                    return ref[pl.ds(pl.multiple_of(at - start, block), block), :].astype(jnp.float32)

                def place_of(step):
                    if isinstance(step, tuple):
                        return slice(step[0] * width, (step[0] + 1) * width)
                    return pl.ds(pl.multiple_of((here_ref[0] + step) % size * width, width), width)

                @pl.loop(0, (last - first) // block, unroll=4)
                def _(b):
                    at = pl.multiple_of(first + b * block, block)
                    total = jnp.zeros((block, HD), jnp.float32)
                    for _, start, ref in some:
                        x = load(ref, at, start)
                        for c in range(0, width, HD):
                            total = total + x[:, c : c + HD] * x[:, c : c + HD]
                    total = jnp.sum(total, -1, keepdims=True)
                    scale = lax.rsqrt(total * (1.0 / depth) + EPS)
                    for step, start, ref in some:
                        chunk = place_of(step)
                        encoded[pl.ds(at, block), chunk] = (
                            load(ref, at, start) * scale * gain_ref[:, chunk]
                        ).astype(jnp.bfloat16)

            refs_of = [(step, start, ref) for (step, start, _), ref in zip(parts, part_refs)]
            if parts[0][0] is None:
                refs_of = [((p,), 0, part_refs[0].at[p]) for p in range(size)]
            edges = sorted({0, rows} | {start for _, start, _ in refs_of})
            for first, last in zip(edges, edges[1:]):
                group(first, last, [r for r in refs_of if r[1] <= first and last <= r[1] + r[2].shape[0]])

        rows_now = encoded[...]
        key_out[...] = jnp.dot(rows_now, key_ref[...], preferred_element_type=jnp.float32).astype(jnp.bfloat16)
        value_out[...] = jnp.dot(rows_now, value_ref[...], preferred_element_type=jnp.float32).astype(jnp.bfloat16)

    out = jax.ShapeDtypeStruct((rows, columns), jnp.bfloat16)
    return pl.pallas_call(
        body,
        grid=(columns // tile,),
        out_shape=(out, out),
        in_specs=[
            pl.BlockSpec(memory_space=pltpu.SMEM),
            pl.BlockSpec((1, depth), lambda i: (0, 0)),
            pl.BlockSpec((depth, tile), lambda i: (0, i)),
            pl.BlockSpec((depth, tile), lambda i: (0, i)),
        ]
        + [pl.BlockSpec(x.shape, lambda i, n=x.ndim: (0,) * n) for _, _, x in parts],
        out_specs=(pl.BlockSpec((rows, tile), lambda i: (0, i)), pl.BlockSpec((rows, tile), lambda i: (0, i))),
        scratch_shapes=[pltpu.VMEM((rows, depth), jnp.bfloat16)],
        compiler_params=pltpu.CompilerParams(vmem_limit_bytes=KERNEL_VMEM),
        cost_estimate=pl.CostEstimate(
            flops=4 * rows * depth * columns, bytes_accessed=4 * depth * columns + 2 * rows * depth, transcendentals=0
        ),
        name="norm_and_project",
    )(here, gain.reshape(1, depth), key_matrix, value_matrix, *[x for _, _, x in parts])


def attend(queries, keys, values, counts):
    stretches = counts.shape[0]
    tokens, width = queries.shape
    stretch = tokens // stretches
    heads = width // HD
    spans = [k.shape[1] for k in keys]
    span = sum(spans)
    n = len(keys)

    per = 3

    def body(count_ref, query_ref, *refs):
        key_refs, value_refs, out_ref = refs[:n], refs[n : 2 * n], refs[2 * n]
        column = lax.broadcasted_iota(jnp.int32, (1, span), 1)
        neighbour = jnp.zeros((1, span), jnp.int32)
        start = 0
        for s in spans:
            for k in range(1, NBR):
                low = start + k * (s // NBR)
                neighbour = jnp.where((column >= low) & (column < low + s // NBR), k, neighbour)
            start += s
        at = [slice(h * HD, (h + 1) * HD) for h in range(heads)]
        for c in range(per):
            row = slice(c * stretch, (c + 1) * stretch)
            kept = neighbour < count_ref[pl.program_id(0) * per + c]
            scores = []
            for a in at:
                k = jnp.concatenate([r[c, :, a] for r in key_refs], 0)
                scores.append(
                    lax.dot_general(
                        query_ref[row, a], k, (((1,), (1,)), ((), ())), preferred_element_type=jnp.float32
                    )
                )
            scores = jnp.concatenate(scores, 0) * HD ** (-0.5)
            scores = jnp.where(kept, scores, -1e30)
            exponents = jnp.exp(scores - jnp.max(scores, -1, keepdims=True))
            weights = (exponents * (1.0 / jnp.sum(exponents, -1, keepdims=True))).astype(jnp.bfloat16)
            for h, a in enumerate(at):
                v = jnp.concatenate([r[c, :, a] for r in value_refs], 0)
                out_ref[row, a] = jnp.dot(
                    weights[h * stretch : (h + 1) * stretch], v, preferred_element_type=jnp.float32
                ).astype(jnp.bfloat16)

    return pl.pallas_call(
        body,
        grid=(stretches // per,),
        out_shape=jax.ShapeDtypeStruct(queries.shape, queries.dtype),
        in_specs=[pl.BlockSpec(memory_space=pltpu.SMEM), pl.BlockSpec((per * stretch, width), lambda c: (c, 0))]
        + [pl.BlockSpec((per, s, width), lambda c: (c, 0, 0)) for s in spans + spans],
        out_specs=pl.BlockSpec((per * stretch, width), lambda c: (c, 0)),
        compiler_params=pltpu.CompilerParams(vmem_limit_bytes=KERNEL_VMEM),
        cost_estimate=pl.CostEstimate(
            flops=4 * tokens * span * width, bytes_accessed=4 * (tokens + stretches * span) * width, transcendentals=tokens * span * heads
        ),
        name="attention",
    )(counts, queries, *keys, *values)


def per_device(queries, neighbours, norm_gain, key_weight, value_weight, slot_anchor, nbr_count):
    owners = lax.axis_size("section") * lax.axis_size("seq")
    slot_count = slot_anchor.shape[0]
    stretches = nbr_count.shape[0]
    width_part = neighbours.shape[1]
    capacity = 2 * ((slot_count // 2 + owners - 1) // owners)
    cells = owners * capacity

    source = slot_anchor // slot_count
    unit_index = slot_anchor % slot_count
    earlier = (source[None, :] == source[:, None]) & (slot_anchor[None, :] < slot_anchor[:, None])
    rank_among = jnp.sum(earlier.astype(jnp.int32), 1)
    grid_cell = source * capacity + rank_among
    cell_ids = jnp.arange(cells, dtype=jnp.int32)
    cell_match = grid_cell[None, :] == cell_ids[:, None]
    request = jnp.sum(jnp.where(cell_match, unit_index[None, :] + 1, 0), 1) - 1
    asked = lax.all_to_all(
        request.reshape(owners, capacity), OWN, split_axis=0, concat_axis=0, tiled=True
    ).reshape(cells)
    units = jnp.arange(slot_count, dtype=jnp.int32)
    position = jnp.max(jnp.where(asked[None, :] == units[:, None], cell_ids[None, :], 0), 1)

    pieces = neighbours.reshape(slot_count, PIECE, width_part)
    starts = [sum(CHUNKS[:j]) for j in range(len(CHUNKS))]
    count = len(CHUNKS)
    size = lax.axis_size("tp")

    def pick(j):
        return scatter_rows(position, pieces, starts[j], CHUNKS[j], cells).reshape(
            owners, capacity, CHUNKS[j], width_part
        )

    def place(j, arrived):
        return gather_rows(grid_cell, arrived.reshape(cells, CHUNKS[j], width_part)).reshape(-1, width_part)

    def shape_rows(x):
        return x.reshape(stretches, -1, x.shape[1])

    parts, done, halves = [], {}, {}

    def finish(j):
        done[j] = project(parts[j], norm_gain, key_weight[0], value_weight[0])

    picked = [pick(j) for j in range(count)]
    for j in range(count):
        ready = picked[j]
        if j >= 2:
            ready = after(ready, parts[j - 2][0][2])
        if j == 3:
            finish(0)
            ready = after(ready, done[0][0])
        arrived = lax.all_to_all(ready, OWN, split_axis=0, concat_axis=0, tiled=True)
        if j == 0:
            arrived = after(arrived, *picked[1:])
        if j - 1 in halves:
            arrived = after(arrived, *halves[j - 1])
        own = place(j, arrived)
        if MODE[j] == "offload":
            full = lax.all_gather(own, "tp", axis=0)
            parts.append([(0, 0, own), (None, 0, full)])
            continue
        up, down = send(own, 1), send(own, size - 1)
        if j >= 2:
            parts[j - 1][-1] = parts[j - 1][-1][:2] + (after(parts[j - 1][-1][2], own),)
            finish(j - 1)
            up, down = lax.optimization_barrier((up, down, done[j - 1][0]))[:2]
        half = own.shape[0] // 2
        halves[j] = up[:half], down[half:]
        far = send(halves[j][0], 1), send(halves[j][1], size - 1)
        parts.append([(0, 0, own), (size - 1, 0, up), (1, 0, down), (2, 0, far[0]), (2, half, far[1])])
    for j in range(count):
        if j not in done:
            finish(j)
    keys = [done[j][0] for j in range(count)]
    values = [done[j][1] for j in range(count)]
    keys = [shape_rows(x) for x in keys]
    values = [shape_rows(x) for x in values]
    return attend(queries, keys, values, nbr_count)


def solution(mesh):
    in_specs = (
        P(("section", "seq"), "tp"),
        P(("section", "seq"), "tp"),
        P(),
        P("section", None, "tp"),
        P("section", None, "tp"),
        P(("section", "seq")),
        P(("section", "seq")),
    )
    out_specs = P(("section", "seq"), "tp")
    return jax.shard_map(
        per_device, mesh=mesh, in_specs=in_specs, out_specs=out_specs, check_vma=False
    )
```
